512 devices in a mesh: sec: 2 (over x_lo), lat: 8 (over y, core), lon: 32 (over z, x_hi).
Axes of the slice: x: 4 (x_hi: 2, x_lo: 2; x = x_hi * 2 + x_lo), y: 4, z: 16, core: 2. Of those that a mesh axis runs over, the one named last changes fastest.
Arguments:
- state: bfloat16 [2, 512, 1440, 256], P('sec', 'lat', 'lon'), may hold values from -6 to 6
- wet_mask: int32 [512, 1440], P('lat', 'lon'), may hold values 0 or 1
- tap_offsets: int32 [512, 3, 3], P('lat'), may hold values from -16 to 16
- conv_weight: bfloat16 [2, 9, 256, 256], P('sec'), may hold values from -0.125 to 0.125
- couple_proj: bfloat16 [2, 256, 128], replicated, may hold values from -0.375 to 0.375
- couple_in: bfloat16 [2, 128, 256], P('sec'), may hold values from -0.5 to 0.5
- norm_gain: float32 [2, 256], P('sec'), may hold values from 0.5 to 1.5
- up_weight: bfloat16 [2, 256, 512], P('sec'), may hold values from -0.375 to 0.375
- down_weight: bfloat16 [2, 512, 256], P('sec'), may hold values from -0.25 to 0.25
Outputs:
- new_state: bfloat16 [2, 512, 1440, 256], P('sec', 'lat', 'lon')
The draws below stay inside these ranges and needn't reach their ends.
All inputs are finite; a program needn't handle non-finite values. No bound on the sum of `wet_mask` on one device may be relied on, other than what follows from the above.
Results may differ from the reference program's by a relative error of at most 0.0038.
Values may be sent and summed in bfloat16 or wider, within the bound.
A program may use at most 128 MiB of HBM per device.

```python
import jax
import jax.numpy as jnp
from jax import lax

C = 256
K = 128
HID = 512
HALO = 16
NLAT = 512
NLON = 1440


def set_ends(entries, stream_key, smallest, top_value):
    spot = [jax.random.randint(jax.random.fold_in(stream_key, axis), (), 0, length) for axis, length in enumerate(entries.shape)]
    widest = entries.shape.index(max(entries.shape))
    next_to = spot[:widest] + [(spot[widest] + 1) % entries.shape[widest]] + spot[widest + 1:]
    return entries.at[tuple(spot)].set(smallest).at[tuple(next_to)].set(top_value)


def levels(key, dims, cuts, low, largest):
    factor_of, own = 1.0, jax.random.fold_in(key, 6)
    for axis_at, blocks in cuts:
        draws = jnp.exp(jax.random.uniform(jax.random.fold_in(own, axis_at), (blocks,), jnp.float32, low / len(cuts), largest / len(cuts)))
        factor_of = factor_of * jnp.repeat(draws, dims[axis_at] // blocks).reshape([-1 if axis == axis_at else 1 for axis in range(len(dims))])
    return factor_of


def bell_draw(own_key, extent, spread, limit, cuts=(), kind=jnp.bfloat16):
    values = spread * jax.random.normal(own_key, extent, jnp.float32)
    if cuts:
        values = values * levels(own_key, extent, cuts, -0.22, 0.18)
    return jnp.clip(values, -limit, limit).astype(kind)


def setup_inputs(seed: int = 0) -> dict:
    streams_of = jax.random.split(jax.random.key(seed), 10)
    state = bell_draw(streams_of[0], (2, NLAT, NLON, C), 1.0, 6.0, ((0, 2), (1, 8), (2, 32)))
    wet_mask = set_ends((jax.random.randint(streams_of[1], (NLAT, NLON), 0, 3) < 2).astype(jnp.int32), jax.random.fold_in(streams_of[1], 1), 0, 1)
    tap_offsets = set_ends(jax.random.randint(streams_of[2], (NLAT, 3, 3), -HALO, HALO + 1), jax.random.fold_in(streams_of[2], 1), -HALO, HALO).astype(jnp.int32)
    conv_weight = bell_draw(streams_of[3], (2, 9, C, C), (9 * C) ** -0.5, 0.125, ((0, 2),))
    couple_proj = bell_draw(streams_of[4], (2, C, K), C ** -0.5, 0.375)
    couple_in = bell_draw(streams_of[5], (2, K, C), K ** -0.5, 0.5, ((0, 2),))
    norm_gain = jnp.clip(1.0 + 0.1 * jax.random.normal(streams_of[6], (2, C), jnp.float32), 0.5, 1.5)
    up_weight = bell_draw(streams_of[7], (2, C, HID), C ** -0.5, 0.375, ((0, 2),))
    down_weight = bell_draw(streams_of[8], (2, HID, C), HID ** -0.5, 0.25, ((0, 2),))
    return {"state": state, "wet_mask": wet_mask, "tap_offsets": tap_offsets, "conv_weight": conv_weight, "couple_proj": couple_proj, "couple_in": couple_in, "norm_gain": norm_gain, "up_weight": up_weight, "down_weight": down_weight}


def reference(state, wet_mask, tap_offsets, conv_weight, couple_proj, couple_in, norm_gain, up_weight, down_weight):
    wet = wet_mask.astype(jnp.float32)
    keeps = [jnp.ones_like(wet), wet]
    features = []
    for sect in range(2):
        proj = jnp.einsum('ijc,ck->ijk', state[sect].astype(jnp.float32), couple_proj[sect].astype(jnp.float32))
        features.append((jax.nn.silu(proj) * keeps[sect][:, :, None]).astype(jnp.bfloat16))
    columns = jnp.arange(NLON, dtype=jnp.int32)
    outputs = []
    for sect in range(2):
        field = state[sect]
        padded = jnp.pad(field, ((1, 1), (0, 0), (0, 0)))
        acc = jnp.zeros((NLAT, NLON, C), jnp.float32)
        for shift_row in range(3):
            band = padded[shift_row:shift_row + NLAT]
            for tap in range(3):
                index = (columns[None, :] + tap_offsets[:, shift_row, tap][:, None]) % NLON
                picked = jnp.take_along_axis(band, index[:, :, None].astype(jnp.int32), axis=1)
                acc = acc + jnp.einsum('ijc,cd->ijd', picked.astype(jnp.float32), conv_weight[sect, 3 * shift_row + tap].astype(jnp.float32))
        other = 1 - sect
        pre = acc + jnp.einsum('ijk,kc->ijc', features[other].astype(jnp.float32), couple_in[sect].astype(jnp.float32))
        meansq = lax.optimization_barrier(jnp.mean(pre * pre, axis=-1, keepdims=True))
        normed = (pre / jnp.sqrt(meansq + 1e-05) * norm_gain[sect]).astype(jnp.bfloat16)
        hidden = jax.nn.gelu(jnp.einsum('ijc,ch->ijh', normed.astype(jnp.float32), up_weight[sect].astype(jnp.float32))).astype(jnp.bfloat16)
        update = jnp.einsum('ijh,hc->ijc', hidden.astype(jnp.float32), down_weight[sect].astype(jnp.float32))
        outputs.append((field.astype(jnp.float32) + keeps[sect][:, :, None] * update).astype(jnp.bfloat16))
    return jnp.stack(outputs, axis=0)
```

```python
import functools
import math

import jax
import jax.numpy as jnp
from jax import lax
from jax.experimental import pallas as pl
from jax.experimental.pallas import tpu as pltpu
from jax.sharding import PartitionSpec as P

HALO = 16
ROWS = 64
COLS = 45
SLOTS = 48
EXT = SLOTS + 2 * HALO
C = 256
K = 128
HID = 512
STEP = 8
STEPS = ROWS // STEP
TAPS = 9
MESH = pl.DeviceIdType.MESH


def kernel(
    x_ref,
    wet_ref,
    off_ref,
    cw_ref,
    cp_ref,
    ci_ref,
    gain_ref,
    up_ref,
    down_ref,
    out_ref,
    ext,
    raw_l,
    raw_r,
    mid_out,
    mid_in,
    diff,
    wet_q,
    picks,
    load_sem,
    s1_send,
    s1_recv,
    s2_send,
    s2_recv,
    f_send,
    f_recv,
    lat_send,
    lat_recv,
):
    sec = lax.axis_index("sec")
    la = lax.axis_index("lat")
    lo = lax.axis_index("lon")
    n_lat = lax.axis_size("lat")
    n_lon = lax.axis_size("lon")
    other = 1 - sec
    west, east = lax.rem(lo + n_lon - 1, n_lon), lax.rem(lo + 1, n_lon)
    north, south = lax.rem(la + n_lat - 1, n_lat), lax.rem(la + 1, n_lat)
    partner = (other, la, lo)
    to_west = (other, la, west)
    to_east = (other, la, east)
    to_north = (sec, north, lo)
    to_south = (sec, south, lo)

    load = pltpu.make_async_copy(x_ref, ext.at[pl.ds(1, ROWS), pl.ds(HALO, SLOTS)], load_sem)
    load.start()

    barrier = pltpu.get_barrier_semaphore()
    for peer in (partner, to_west, to_east, to_north, to_south):
        pl.semaphore_signal(barrier, inc=1, device_id=peer, device_id_type=MESH)

    def rows_of(c):
        if isinstance(c, int) and c < 2:
            return pl.ds(1 if c == 0 else ROWS, 1)
        if isinstance(c, int) and c == STEPS + 1:
            return pl.ds(2 + STEP * (c - 2), STEP - 2)
        return pl.ds(2 + STEP * (c - 2), STEP)

    def first_hop(c):
        rows = rows_of(c)
        return [
            pltpu.make_async_remote_copy(
                src_ref=ext.at[rows, pl.ds(start, HALO)],
                dst_ref=buf.at[rows],
                send_sem=s1_send.at[side, c],
                recv_sem=s1_recv.at[side, c],
                device_id=partner,
                device_id_type=MESH,
            )
            for side, (buf, start) in enumerate(((raw_l, HALO), (raw_r, SLOTS)))
        ]

    def second_hop(c):
        rows = rows_of(c)
        return [
            pltpu.make_async_remote_copy(
                src_ref=buf.at[rows],
                dst_ref=ext.at[rows, pl.ds(start, HALO)],
                send_sem=s2_send.at[side, c],
                recv_sem=s2_recv.at[side, c],
                device_id=target,
                device_id_type=MESH,
            )
            for side, (buf, start, target) in enumerate(
                ((raw_l, HALO + SLOTS, to_west), (raw_r, 0, to_east))
            )
        ]

    def features_hop(c):
        rows = pl.ds(STEP * c, STEP)
        return pltpu.make_async_remote_copy(
            src_ref=mid_out.at[rows],
            dst_ref=mid_in.at[rows],
            send_sem=f_send.at[c],
            recv_sem=f_recv.at[c],
            device_id=partner,
            device_id_type=MESH,
        )

    def lat_hop(side):
        src, dst, target = ((1, ROWS + 1, to_north), (ROWS, 0, to_south))[side]
        return pltpu.make_async_remote_copy(
            src_ref=ext.at[src],
            dst_ref=ext.at[dst],
            send_sem=lat_send.at[side],
            recv_sem=lat_recv.at[side],
            device_id=target,
            device_id_type=MESH,
        )

    slot = lax.broadcasted_iota(jnp.int32, (SLOTS, 3 * EXT), 0)
    pos = lax.broadcasted_iota(jnp.int32, (SLOTS, 3 * EXT), 1)
    slot_col = jnp.where(slot < 32, slot, slot - 3)
    for dy in range(3):
        at = pos - EXT * dy
        col = jnp.where(at < HALO + 29, at - HALO, at - HALO - 3)
        good = (at >= 0) & (at < EXT) & ((at < HALO + 29) | (at >= HALO + 32))
        diff[dy] = jnp.where(good, col - slot_col, 1000)

    q_col = lax.broadcasted_iota(jnp.int32, (SLOTS, COLS), 0)
    q_col = jnp.where(q_col < 32, q_col, q_col - 3)
    to_slot = (q_col == lax.broadcasted_iota(jnp.int32, (SLOTS, COLS), 1)).astype(jnp.bfloat16)
    wet_q[...] = jnp.dot(
        to_slot,
        wet_ref[...].astype(jnp.float32).astype(jnp.bfloat16),
        preferred_element_type=jnp.float32,
    ).astype(jnp.bfloat16)

    def silu(v):
        return v * (0.5 + 0.5 * jnp.tanh(0.5 * v))

    def compute(c):
        base = c * STEP

        @pl.loop(0, STEP)
        def _(i):
            window = ext[pl.ds(base + i, 3)].reshape(3 * EXT, C)
            select = jnp.concatenate(
                [
                    jnp.where(diff[t // 3] == off_ref[t // 3, t % 3, base + i], 1.0, 0.0).astype(jnp.bfloat16)
                    for t in range(TAPS)
                ],
                axis=0,
            )
            picked = jnp.dot(select, window, preferred_element_type=jnp.float32).astype(jnp.bfloat16)
            start = pl.multiple_of(i * SLOTS, 16)
            for t in range(TAPS):
                picks[pl.ds(start, SLOTS), t * C : (t + 1) * C] = picked[t * SLOTS : (t + 1) * SLOTS]

        cells = STEP * SLOTS
        acc = jnp.dot(picks[...], cw_ref[...], preferred_element_type=jnp.float32)

        rows = lax.broadcasted_iota(jnp.int32, (ROWS, STEP * K), 0)
        lanes = lax.broadcasted_iota(jnp.int32, (ROWS, STEP * K), 1)
        spread = (rows == base + lanes // K).astype(jnp.bfloat16)
        wet = jnp.dot(wet_q[...], spread, preferred_element_type=jnp.float32)
        wet = jnp.concatenate([wet[:, i * K : (i + 1) * K] for i in range(STEP)], axis=0)
        keep_own = jnp.where(sec == 0, 1.0, wet)
        keep_other = jnp.where(sec == 0, wet, 1.0)

        edge = jnp.concatenate(
            [raw_l[pl.ds(base + 1, STEP)], raw_r[pl.ds(base + 1, STEP)]], axis=1
        ).reshape(STEP * 2 * HALO, C)
        edge = silu(jnp.dot(edge, cp_ref[other], preferred_element_type=jnp.float32))
        edge = edge.reshape(STEP, 2 * HALO, K)
        mid = mid_in[pl.ds(base, STEP)].astype(jnp.float32)
        feat = jnp.concatenate([edge[:, :HALO], mid, edge[:, HALO:]], axis=1).reshape(cells, K)
        feat = (feat * keep_other).astype(jnp.bfloat16)
        pre = acc + jnp.dot(feat, ci_ref[...], preferred_element_type=jnp.float32)

        meansq = jnp.mean(pre * pre, axis=-1, keepdims=True)
        normed = (pre * lax.rsqrt(meansq + 1e-05) * gain_ref[...]).astype(jnp.bfloat16)
        h = jnp.dot(normed, up_ref[...], preferred_element_type=jnp.float32)
        h = 0.5 * h * (1.0 + jnp.tanh(math.sqrt(2.0 / math.pi) * (h + 0.044715 * (h * h * h))))
        update = jnp.dot(h.astype(jnp.bfloat16), down_ref[...], preferred_element_type=jnp.float32)
        update = update * jnp.concatenate([keep_own, keep_own], axis=1)
        field = ext[pl.ds(base + 1, STEP), HALO : HALO + SLOTS].astype(jnp.float32)
        out_ref[pl.ds(base, STEP)] = (field + update.reshape(STEP, SLOTS, C)).astype(jnp.bfloat16)

    load.wait()
    pl.semaphore_wait(barrier, 5)

    def start(copies):
        for copy in copies:
            copy.start()

    for c in range(STEPS + 2):
        start(first_hop(c))

    @pl.loop(0, STEPS)
    def _(c):
        own = ext[pl.ds(c * STEP + 1, STEP), 2 * HALO : 3 * HALO].reshape(STEP * HALO, C)
        own = silu(jnp.dot(own, cp_ref[sec], preferred_element_type=jnp.float32))
        mid_out[pl.ds(c * STEP, STEP)] = own.astype(jnp.bfloat16).reshape(STEP, HALO, K)
        features_hop(c).start()

    def relay(c):
        for arrived, onward in zip(first_hop(c), second_hop(c)):
            arrived.wait_recv()
            onward.start()

    def halo_wait(c):
        for copy in second_hop(c):
            copy.wait_recv()

    relay(0)
    relay(1)
    relay(2)
    halo_wait(0)
    halo_wait(1)
    lat_hop(0).start()
    lat_hop(1).start()

    @pl.loop(0, STEPS)
    def _(c):
        @pl.when(c < STEPS - 2)
        def _():
            relay(c + 3)

        @pl.when(c == STEPS - 2)
        def _():
            relay(STEPS + 1)

        @pl.when(c < STEPS - 1)
        def _():
            halo_wait(c + 2)

        @pl.when(c == STEPS - 1)
        def _():
            halo_wait(STEPS + 1)
            lat_hop(0).wait_recv()

            @pl.when(la == n_lat - 1)
            def _():
                ext[ROWS + 1] = jnp.zeros((EXT, C), jnp.bfloat16)

        @pl.when(c == 0)
        def _():
            lat_hop(1).wait_recv()

            @pl.when(la == 0)
            def _():
                ext[0] = jnp.zeros((EXT, C), jnp.bfloat16)

        features_hop(c).wait_recv()
        compute(c)

    for c in range(STEPS + 2):
        for copy in first_hop(c) + second_hop(c):
            copy.wait_send()
    for c in range(STEPS):
        features_hop(c).wait_send()
    lat_hop(0).wait_send()
    lat_hop(1).wait_send()


def local(state, wet_mask, tap_offsets, conv_weight, couple_proj, couple_in, norm_gain, up_weight, down_weight):
    x = state[0]
    x = jnp.concatenate([x[:, :32], x[:, 29:]], axis=1)
    vmem = pl.BlockSpec(memory_space=pltpu.VMEM)
    dma = pltpu.SemaphoreType.DMA
    out = pl.pallas_call(
        kernel,
        out_shape=jax.ShapeDtypeStruct((ROWS, SLOTS, C), jnp.bfloat16),
        in_specs=[pl.BlockSpec(memory_space=pl.ANY), vmem, pl.BlockSpec(memory_space=pltpu.SMEM)] + [vmem] * 6,
        out_specs=vmem,
        scratch_shapes=[
            pltpu.VMEM((ROWS + 2, EXT, C), jnp.bfloat16),
            pltpu.VMEM((ROWS + 2, HALO, C), jnp.bfloat16),
            pltpu.VMEM((ROWS + 2, HALO, C), jnp.bfloat16),
            pltpu.VMEM((ROWS, HALO, K), jnp.bfloat16),
            pltpu.VMEM((ROWS, HALO, K), jnp.bfloat16),
            pltpu.VMEM((3, SLOTS, 3 * EXT), jnp.int32),
            pltpu.VMEM((SLOTS, ROWS), jnp.bfloat16),
            pltpu.VMEM((STEP * SLOTS, TAPS * C), jnp.bfloat16),
            dma,
            dma((2, STEPS + 2)),
            dma((2, STEPS + 2)),
            dma((2, STEPS + 2)),
            dma((2, STEPS + 2)),
            dma((STEPS,)),
            dma((STEPS,)),
            dma((2,)),
            dma((2,)),
        ],
        compiler_params=pltpu.CompilerParams(
            collective_id=0, has_side_effects=True, vmem_limit_bytes=48 * 1024 * 1024
        ),
        cost_estimate=pl.CostEstimate(flops=8_000_000_000, bytes_accessed=5_000_000, transcendentals=2_000_000),
    )(
        x,
        wet_mask.T,
        tap_offsets.transpose(1, 2, 0),
        conv_weight[0].reshape(TAPS * C, C),
        couple_proj,
        couple_in[0],
        norm_gain,
        up_weight[0],
        down_weight[0],
    )
    return jnp.concatenate([out[:, :29], out[:, 32:]], axis=1)[None]


def solution(mesh):
    in_specs = (
        P("sec", "lat", "lon", None),
        P("lat", "lon"),
        P("lat", None, None),
        P("sec", None, None, None),
        P(),
        P("sec", None, None),
        P("sec", None),
        P("sec", None, None),
        P("sec", None, None),
    )
    out_specs = P("sec", "lat", "lon", None)
    return jax.shard_map(local, mesh=mesh, in_specs=in_specs, out_specs=out_specs, check_vma=False)
```

```python
import math

import jax
import jax.numpy as jnp
from jax import lax
from jax.experimental import pallas as pl
from jax.experimental.pallas import tpu as pltpu
from jax.sharding import PartitionSpec as P

HALO = 16
ROWS = 64
COLS = 45
SLOTS = 48
EXT = 82
C = 256
K = 128
HID = 512
STEP = 8
STEPS = ROWS // STEP
CHUNKS = STEPS + 2
AHEAD = 2
LEAD = 4
COL_UNROLL = 5
GROUP = 16
TAPS = 9
MESH = pl.DeviceIdType.MESH


def kernel(
    x_hbm,
    wet_hbm,
    off_hbm,
    cw_hbm,
    cp_hbm,
    ci_hbm,
    gain_hbm,
    up_hbm,
    down_hbm,
    out_ref,
    x_ref,
    wet_ref,
    off_ref,
    cw_ref,
    cp_ref,
    ci_ref,
    gain_ref,
    up_ref,
    down_ref,
    wide,
    own_l,
    own_m,
    own_r,
    raw_l,
    raw_r,
    halo_l,
    halo_r,
    lat_out,
    lat_in,
    mid_out,
    mid_in,
    feat,
    wet_q,
    picks,
    load_sem,
    s1_send,
    s1_recv,
    s2_send,
    s2_recv,
    f_send,
    f_recv,
    lat_send,
    lat_recv,
):
    sec = lax.axis_index("sec")
    la = lax.axis_index("lat")
    lo = lax.axis_index("lon")
    n_lat = lax.axis_size("lat")
    n_lon = lax.axis_size("lon")
    other = 1 - sec
    west, east = lax.rem(lo + n_lon - 1, n_lon), lax.rem(lo + 1, n_lon)
    north, south = lax.rem(la + n_lat - 1, n_lat), lax.rem(la + 1, n_lat)
    partner = (other, la, lo)
    to_west = (other, la, west)
    to_east = (other, la, east)
    to_north = (sec, north, lo)
    to_south = (sec, south, lo)

    barrier = pltpu.get_barrier_semaphore()
    for peer in (partner, to_west, to_east, to_north, to_south):
        pl.semaphore_signal(barrier, inc=1, device_id=peer, device_id_type=MESH)

    loads = [
        pltpu.make_async_copy(src, dst, load_sem.at[i])
        for i, (src, dst) in enumerate(
            (
                (x_hbm, x_ref),
                (cp_hbm, cp_ref),
                (wet_hbm, wet_ref),
                (off_hbm, off_ref),
                (ci_hbm, ci_ref),
                (gain_hbm, gain_ref),
                (cw_hbm, cw_ref),
                (up_hbm, up_ref),
                (down_hbm, down_ref),
            )
        )
    ]
    for copy in loads:
        copy.start()

    def rows_of(c):
        if isinstance(c, int) and c < 2:
            return pl.ds(1 if c == 0 else ROWS, 1)
        if isinstance(c, int) and c == CHUNKS - 1:
            return pl.ds(2 + STEP * (c - 2), STEP - 2)
        return pl.ds(2 + STEP * (c - 2), STEP)

    def hop(c, pairs, targets, send_sem, recv_sem):
        rows = rows_of(c)
        return [
            pltpu.make_async_remote_copy(
                src_ref=src.at[rows],
                dst_ref=dst.at[rows],
                send_sem=send_sem.at[side, c],
                recv_sem=recv_sem.at[side, c],
                device_id=targets[side],
                device_id_type=MESH,
            )
            for side, (src, dst) in enumerate(pairs)
        ]

    def first_hop(c):
        return hop(c, ((own_l, raw_l), (own_r, raw_r)), (partner, partner), s1_send, s1_recv)

    def second_hop(c):
        return hop(c, ((raw_l, halo_r), (raw_r, halo_l)), (to_west, to_east), s2_send, s2_recv)

    def features_hop(c):
        rows = pl.ds(STEP * c, STEP)
        return pltpu.make_async_remote_copy(
            src_ref=mid_out.at[rows],
            dst_ref=mid_in.at[rows],
            send_sem=f_send.at[c],
            recv_sem=f_recv.at[c],
            device_id=partner,
            device_id_type=MESH,
        )

    def lat_hop(side):
        return pltpu.make_async_remote_copy(
            src_ref=lat_out.at[side],
            dst_ref=lat_in.at[side],
            send_sem=lat_send.at[side],
            recv_sem=lat_recv.at[side],
            device_id=(to_north, to_south)[side],
            device_id_type=MESH,
        )

    def silu(v):
        return v * (0.5 + 0.5 * jnp.tanh(0.5 * v))

    def at(row, half, col):
        return (row * 2 + half) * EXT + col

    halves = [slice(half * 128, half * 128 + 128) for half in range(2)]

    def to_rows(g):
        base = g * GROUP

        @pl.loop(0, COLS, unroll=COL_UNROLL)
        def _(col):
            x = x_ref[col, pl.ds(pl.multiple_of(base, GROUP), GROUP)].astype(jnp.float32)
            for half in range(2):
                wide[pl.ds(at(base + 1, half, HALO + col), GROUP, 2 * EXT), :] = x[:, halves[half]]

        @pl.loop(0, GROUP, unroll=2)
        def _(i):
            row = base + 1 + i
            for half in range(2):
                for dst, col in ((own_l, 0), (own_m, 16), (own_r, COLS - HALO)):
                    dst[row, :, halves[half]] = wide[pl.ds(at(row, half, HALO + col), HALO), :].astype(jnp.bfloat16)

    def widen(start, rows):
        for row in range(rows):
            for half in range(2):
                for src, col in ((halo_l, 0), (halo_r, HALO + COLS)):
                    x = src[start + row, :, halves[half]]
                    wide[pl.ds(at(start + row, half, col), HALO), :] = x.astype(jnp.float32)

    def start(copies):
        for copy in copies:
            copy.start()

    def relay(c):
        for arrived, onward in zip(first_hop(c), second_hop(c)):
            arrived.wait_recv()
            onward.start()

    def sent(c):
        for copy in first_hop(c):
            copy.wait_send()

    def pass_on(c):
        relay(c)
        sent(c)
        start(first_hop(c + AHEAD))

    def halo_wait(c):
        for copy in second_hop(c):
            copy.wait_recv()

    def lat_row(side, real):
        row = (ROWS + 1, 0)[side]
        for half in range(2):
            x = lat_in[side, 0:EXT, halves[half]].astype(jnp.float32)
            wide[pl.ds(at(row, half, 0), EXT), :] = jnp.where(real, x, 0.0)

    def compute(c):
        base = c * STEP
        cells = STEP * SLOTS

        @pl.loop(0, STEP)
        def _(i):
            start = pl.multiple_of(i * SLOTS, 16)
            for t in range(TAPS):
                first = off_ref[t // 3, t % 3, base + i] + HALO
                for half in range(2):
                    picked = wide[pl.ds(at(base + i + t // 3, half, first), SLOTS), :]
                    lanes = slice(t * C + half * 128, t * C + half * 128 + 128)
                    picks[pl.ds(start, SLOTS), lanes] = picked.astype(jnp.bfloat16)

        acc = jnp.dot(picks[...], cw_ref[...], preferred_element_type=jnp.float32)

        rows = lax.broadcasted_iota(jnp.int32, (ROWS, STEP * K), 0)
        lanes = lax.broadcasted_iota(jnp.int32, (ROWS, STEP * K), 1)
        spread = (rows == base + lanes // K).astype(jnp.bfloat16)
        wet = jnp.dot(wet_q[...], spread, preferred_element_type=jnp.float32)
        wet = jnp.concatenate([wet[:, i * K : (i + 1) * K] for i in range(STEP)], axis=0)
        keep_own = jnp.where(sec == 0, 0.5, 0.5 * wet)
        keep_other = jnp.where(sec == 0, wet, 1.0)

        edge = jnp.concatenate(
            [raw_l[pl.ds(base + 1, STEP)], raw_r[pl.ds(base + 1, STEP)]], axis=1
        ).reshape(STEP * 2 * HALO, C)
        edge = silu(jnp.dot(edge, cp_ref[other], preferred_element_type=jnp.float32))
        edge = edge.reshape(STEP, 2 * HALO, K)
        feat[:, 0:16] = edge[:, :HALO]
        feat[:, 16:32] = mid_in[pl.ds(base, STEP)].astype(jnp.float32)
        feat[:, 29:45] = edge[:, HALO:]
        coupled = (feat[...].reshape(cells, K) * keep_other).astype(jnp.bfloat16)
        pre = acc + jnp.dot(coupled, ci_ref[...], preferred_element_type=jnp.float32)

        meansq = jnp.mean(pre * pre, axis=-1, keepdims=True)
        normed = (pre * lax.rsqrt(meansq + 1e-05) * gain_ref[...]).astype(jnp.bfloat16)
        h = jnp.dot(normed, up_ref[...], preferred_element_type=jnp.float32)
        s2p = math.sqrt(2.0 / math.pi)
        h = h + h * jnp.tanh(h * (s2p + (s2p * 0.044715) * (h * h)))
        update = jnp.dot(h.astype(jnp.bfloat16), down_ref[...], preferred_element_type=jnp.float32)
        update = update * jnp.concatenate([keep_own, keep_own], axis=1)
        field = [
            jnp.concatenate([wide[pl.ds(at(base + 1 + i, half, HALO), SLOTS), :] for i in range(STEP)], axis=0)
            for half in range(2)
        ]
        result = (jnp.concatenate(field, axis=1) + update).reshape(STEP, SLOTS, C)
        out_ref[pl.ds(base, STEP)] = result[:, :COLS].astype(jnp.bfloat16)

    loads[0].wait()
    last = ROWS // GROUP - 1
    to_rows(0)
    to_rows(last)
    pl.semaphore_wait(barrier, 5)
    for c in range(2 + min(AHEAD, GROUP // STEP - 1)):
        start(first_hop(c))

    @pl.loop(1, last)
    def _(g):
        to_rows(g)

    for c in range(2 + min(AHEAD, GROUP // STEP - 1), 2 + AHEAD):
        start(first_hop(c))

    loads[1].wait()

    @pl.loop(0, ROWS // GROUP)
    def _(g):
        own = own_m[pl.ds(g * GROUP + 1, GROUP)].reshape(GROUP * HALO, C)
        own = silu(jnp.dot(own, cp_ref[sec], preferred_element_type=jnp.float32))
        mid_out[pl.ds(g * GROUP, GROUP)] = own.astype(jnp.bfloat16).reshape(GROUP, HALO, K)

    features_hop(0).start()

    loads[2].wait()
    to_slot = lax.broadcasted_iota(jnp.int32, (SLOTS, COLS), 0) == lax.broadcasted_iota(jnp.int32, (SLOTS, COLS), 1)
    wet_q[...] = jnp.dot(
        to_slot.astype(jnp.bfloat16),
        wet_ref[...].astype(jnp.float32).astype(jnp.bfloat16),
        preferred_element_type=jnp.float32,
    ).astype(jnp.bfloat16)
    feat[...] = jnp.zeros_like(feat)

    @pl.loop(0, (ROWS + 2) * 2)
    def _(i):
        wide[pl.ds(i * EXT + 77, 5), :] = jnp.zeros((5, 128), jnp.float32)

    for copy in loads[3:]:
        copy.wait()

    relay(0)
    relay(1)
    pass_on(2)
    halo_wait(0)
    halo_wait(1)
    for side, row in enumerate((1, ROWS)):
        widen(row, 1)
        for half in range(2):
            lat_out[side, 0:EXT, halves[half]] = wide[pl.ds(at(row, half, 0), EXT), :].astype(jnp.bfloat16)
        lat_hop(side).start()
    for c in range(3, LEAD):
        pass_on(c)

    @pl.loop(0, STEPS)
    def _(c):
        @pl.when(c < CHUNKS - 1 - LEAD)
        def _():
            relay(c + LEAD)
            sent(c + LEAD)

        @pl.when(c < CHUNKS - 1 - LEAD - AHEAD)
        def _():
            start(first_hop(c + LEAD + AHEAD))

        @pl.when(c == CHUNKS - 1 - LEAD - AHEAD)
        def _():
            start(first_hop(CHUNKS - 1))

        @pl.when(c < STEPS - 1)
        def _():
            features_hop(c + 1).start()

        @pl.when(c == CHUNKS - 1 - LEAD)
        def _():
            relay(CHUNKS - 1)
            sent(CHUNKS - 1)

        @pl.when(c < STEPS - 1)
        def _():
            halo_wait(c + 2)
            widen(STEP * c + 2, STEP)

        @pl.when(c == STEPS - 1)
        def _():
            halo_wait(CHUNKS - 1)
            widen(2 + STEP * (STEPS - 1), STEP - 2)
            lat_hop(0).wait_recv()
            lat_row(0, la < n_lat - 1)

        @pl.when(c == 0)
        def _():
            lat_hop(1).wait_recv()
            lat_row(1, la > 0)

        features_hop(c).wait_recv()
        compute(c)

    sent(0)
    sent(1)
    for c in range(CHUNKS):
        for copy in second_hop(c):
            copy.wait_send()
    for c in range(STEPS):
        features_hop(c).wait_send()
    lat_hop(0).wait_send()
    lat_hop(1).wait_send()


def local(state, wet_mask, tap_offsets, conv_weight, couple_proj, couple_in, norm_gain, up_weight, down_weight):
    args = (
        state[0].transpose(1, 0, 2),
        wet_mask.T,
        tap_offsets.transpose(1, 2, 0),
        conv_weight[0].reshape(TAPS * C, C),
        couple_proj,
        couple_in[0],
        norm_gain,
        up_weight[0],
        down_weight[0],
    )
    dma = pltpu.SemaphoreType.DMA
    edge = pltpu.VMEM((ROWS + 2, HALO, C), jnp.bfloat16)
    out = pl.pallas_call(
        kernel,
        out_shape=jax.ShapeDtypeStruct((ROWS, COLS, C), jnp.bfloat16),
        in_specs=[pl.BlockSpec(memory_space=pltpu.HBM)] * len(args),
        out_specs=pl.BlockSpec(memory_space=pltpu.VMEM),
        scratch_shapes=[(pltpu.SMEM if i == 2 else pltpu.VMEM)(a.shape, a.dtype) for i, a in enumerate(args)]
        + [
            pltpu.VMEM(((ROWS + 2) * 2 * EXT, 128), jnp.float32),
        ]
        + [edge] * 7
        + [
            pltpu.VMEM((2, 96, C), jnp.bfloat16),
            pltpu.VMEM((2, 96, C), jnp.bfloat16),
            pltpu.VMEM((ROWS, HALO, K), jnp.bfloat16),
            pltpu.VMEM((ROWS, HALO, K), jnp.bfloat16),
            pltpu.VMEM((STEP, SLOTS, K), jnp.float32),
            pltpu.VMEM((SLOTS, ROWS), jnp.bfloat16),
            pltpu.VMEM((STEP * SLOTS, TAPS * C), jnp.bfloat16),
            dma((len(args),)),
            dma((2, CHUNKS)),
            dma((2, CHUNKS)),
            dma((2, CHUNKS)),
            dma((2, CHUNKS)),
            dma((STEPS,)),
            dma((STEPS,)),
            dma((2,)),
            dma((2,)),
        ],
        compiler_params=pltpu.CompilerParams(
            collective_id=0, has_side_effects=True, vmem_limit_bytes=62 * 1024 * 1024
        ),
        cost_estimate=pl.CostEstimate(flops=6_000_000_000, bytes_accessed=5_000_000, transcendentals=2_000_000),
    )(*args)
    return out[None]


def solution(mesh):
    in_specs = (
        P("sec", "lat", "lon", None),
        P("lat", "lon"),
        P("lat", None, None),
        P("sec", None, None, None),
        P(),
        P("sec", None, None),
        P("sec", None),
        P("sec", None, None),
        P("sec", None, None),
    )
    out_specs = P("sec", "lat", "lon", None)
    return jax.shard_map(local, mesh=mesh, in_specs=in_specs, out_specs=out_specs, check_vma=False)
```

```python
import math

import jax
import jax.numpy as jnp
from jax import lax
from jax.experimental import pallas as pl
from jax.experimental.pallas import tpu as pltpu
from jax.sharding import PartitionSpec as P

HALO = 16
ROWS = 64
COLS = 45
EXT = 82
C = 256
K = 128
HID = 512
STEP = 16
STEPS = ROWS // STEP
CHUNKS = STEPS + 2
WIDE = 32
EARLY = 4
LEAD = 4
COL_UNROLL = 5
TAPS = 9
MESH = pl.DeviceIdType.MESH


def kernel(
    x_hbm,
    wet_hbm,
    off_hbm,
    cw_hbm,
    cp_hbm,
    ci_hbm,
    gain_hbm,
    up_hbm,
    down_hbm,
    out_ref,
    x_ref,
    wet_ref,
    off_ref,
    cw_ref,
    cp_ref,
    ci_ref,
    gain_ref,
    up_ref,
    down_ref,
    wide,
    own_far,
    own_mid,
    own_near,
    raw_far,
    raw_near,
    halo_far,
    halo_near,
    lat_out,
    lat_in,
    mid_out,
    mid_in,
    feat,
    wet_far,
    wet_near,
    picks,
    load_sem,
    far_sem,
    near_sem,
    hello,
    f_send,
    f_recv,
    lat_send,
    lat_recv,
):
    sec = lax.axis_index("sec")
    la = lax.axis_index("lat")
    lo = lax.axis_index("lon")
    n_lat = lax.axis_size("lat")
    n_lon = lax.axis_size("lon")
    other = 1 - sec
    odd = lax.rem(lo, 2)
    near = lo + 1 - 2 * odd
    far = lax.rem(lo + n_lon - 1 + 2 * odd, n_lon)
    north, south = lax.rem(la + n_lat - 1, n_lat), lax.rem(la + 1, n_lat)
    partner = (other, la, lo)
    to_near = (other, la, near)
    to_far = (other, la, far)
    to_north = (sec, north, lo)
    to_south = (sec, south, lo)

    barrier = pltpu.get_barrier_semaphore()

    def tell(*peers):
        for peer in peers:
            pl.semaphore_signal(barrier, inc=1, device_id=peer, device_id_type=MESH)

    def greet(i, peer):
        pl.semaphore_signal(hello.at[i], inc=1, device_id=peer, device_id_type=MESH)

    @pl.when(sec == 0)
    def _():
        tell(to_north, to_south, to_far)

    @pl.when(sec == 1)
    def _():
        tell(partner, to_near, to_north, to_south)

    def meet_far():
        pl.semaphore_wait(barrier, 3)
        greet(2, to_far)

    loads = [
        pltpu.make_async_copy(src, dst, load_sem.at[i])
        for i, (src, dst) in enumerate(
            (
                (x_hbm, x_ref),
                (cp_hbm, cp_ref),
                (wet_hbm, wet_ref),
                (off_hbm, off_ref),
                (ci_hbm, ci_ref),
                (gain_hbm, gain_ref),
                (cw_hbm, cw_ref),
                (up_hbm, up_ref),
                (down_hbm, down_ref),
            )
        )
    ]
    for copy in loads:
        copy.start()

    def rows_of(c):
        if isinstance(c, int) and c < 2:
            return pl.ds(1 if c == 0 else ROWS, 1)
        if isinstance(c, int) and c == CHUNKS - 1:
            return pl.ds(2 + STEP * (c - 2), STEP - 2)
        return pl.ds(2 + STEP * (c - 2), STEP)

    def hop(rows, src, dst, sems, first, c, target):
        return pltpu.make_async_remote_copy(
            src_ref=src.at[rows],
            dst_ref=dst.at[rows],
            send_sem=sems.at[first, c],
            recv_sem=sems.at[first + 1, c],
            device_id=target,
            device_id_type=MESH,
        )

    def far_first(c):
        return hop(rows_of(c), own_far, raw_far, far_sem, 0, c, partner)

    def far_second(c):
        return hop(rows_of(c), raw_far, halo_far, far_sem, 2, c, to_far)

    def near_first(c):
        return hop(rows_of(c), own_near, raw_near, near_sem, 0, c, partner)

    def near_second(c):
        return hop(rows_of(c), raw_near, halo_near, near_sem, 2, c, to_near)

    def features_hop(c):
        rows = pl.ds(STEP * c, STEP)
        return pltpu.make_async_remote_copy(
            src_ref=mid_out.at[rows],
            dst_ref=mid_in.at[rows],
            send_sem=f_send.at[c],
            recv_sem=f_recv.at[c],
            device_id=partner,
            device_id_type=MESH,
        )

    def lat_hop(side):
        return pltpu.make_async_remote_copy(
            src_ref=lat_out.at[side],
            dst_ref=lat_in.at[side],
            send_sem=lat_send.at[side],
            recv_sem=lat_recv.at[side],
            device_id=(to_north, to_south)[side],
            device_id_type=MESH,
        )

    def silu(v):
        return v * (0.5 + 0.5 * jnp.tanh(0.5 * v))

    def at(row, half, col):
        return (row * 2 + half) * EXT + col

    far_col, near_col = (COLS - HALO) * odd, (COLS - HALO) * (1 - odd)
    far_at, near_at = (HALO + COLS) * odd, (HALO + COLS) * (1 - odd)
    halves = [slice(half * 128, half * 128 + 128) for half in range(2)]

    def to_rows(g):
        base = g * STEP

        @pl.loop(0, COLS, unroll=COL_UNROLL)
        def _(col):
            x = x_ref[col, pl.ds(pl.multiple_of(base, STEP), STEP)].astype(jnp.float32)
            for half in range(2):
                wide[pl.ds(at(base + 1, half, HALO + col), STEP, 2 * EXT), :] = x[:, halves[half]]

        @pl.loop(0, STEP, unroll=2)
        def _(i):
            row = base + 1 + i
            for half in range(2):
                for dst, col in ((own_far, far_col), (own_mid, 16), (own_near, near_col)):
                    dst[row, :, halves[half]] = wide[pl.ds(at(row, half, HALO + col), HALO), :].astype(jnp.bfloat16)

    def widen(halo, where, start, rows):
        for row in range(rows):
            for half in range(2):
                x = halo[start + row, :, halves[half]]
                wide[pl.ds(at(start + row, half, where), HALO), :] = x.astype(jnp.float32)

    def relay(arrived, onward):
        arrived.wait_recv()
        onward.start()

    def lat_row(side, real):
        row = (ROWS + 1, 0)[side]
        for half in range(2):
            x = lat_in[side, 0:EXT, halves[half]].astype(jnp.float32)
            wide[pl.ds(at(row, half, 0), EXT), :] = jnp.where(real, x, 0.0)

    def edge_features(raw, base):
        x = raw[pl.ds(base + 1, STEP)].reshape(STEP * HALO, C)
        return silu(jnp.dot(x, cp_ref[other], preferred_element_type=jnp.float32))

    def compute(base, cols, first_col, features, wet_of):
        cells = STEP * cols

        @pl.loop(0, STEP)
        def _(i):
            start = pl.multiple_of(i * cols, 16)
            for t in range(TAPS):
                first = off_ref[t // 3, t % 3, base + i] + HALO + first_col
                for half in range(2):
                    picked = wide[pl.ds(at(base + i + t // 3, half, first), cols), :]
                    lanes = slice(t * C + half * 128, t * C + half * 128 + 128)
                    picks[pl.ds(start, cols), lanes] = picked.astype(jnp.bfloat16)

        acc = jnp.dot(picks[0:cells], cw_ref[...], preferred_element_type=jnp.float32)

        rows = lax.broadcasted_iota(jnp.int32, (ROWS, STEP * K), 0)
        lanes = lax.broadcasted_iota(jnp.int32, (ROWS, STEP * K), 1)
        spread = (rows == base + lanes // K).astype(jnp.bfloat16)
        wet = jnp.dot(wet_of[...], spread, preferred_element_type=jnp.float32)
        wet = jnp.concatenate([wet[:, i * K : (i + 1) * K] for i in range(STEP)], axis=0)
        keep_own = jnp.where(sec == 0, 0.5, 0.5 * wet)
        keep_other = jnp.where(sec == 0, wet, 1.0)

        coupled = (features * keep_other).astype(jnp.bfloat16)
        pre = acc + jnp.dot(coupled, ci_ref[...], preferred_element_type=jnp.float32)
        meansq = jnp.mean(pre * pre, axis=-1, keepdims=True)
        normed = (pre * lax.rsqrt(meansq + 1e-05) * gain_ref[...]).astype(jnp.bfloat16)
        h = jnp.dot(normed, up_ref[...], preferred_element_type=jnp.float32)
        s2p = math.sqrt(2.0 / math.pi)
        h = h + h * jnp.tanh(h * (s2p + (s2p * 0.044715) * (h * h)))
        update = jnp.dot(h.astype(jnp.bfloat16), down_ref[...], preferred_element_type=jnp.float32)
        update = update * jnp.concatenate([keep_own, keep_own], axis=1)
        field = [
            jnp.concatenate(
                [wide[pl.ds(at(base + 1 + i, half, HALO + first_col), cols), :] for i in range(STEP)], axis=0
            )
            for half in range(2)
        ]
        return (jnp.concatenate(field, axis=1) + update).astype(jnp.bfloat16).reshape(STEP, cols, C)

    def compute_far(c):
        base = c * STEP
        rows = pl.ds(base, STEP)
        edge = edge_features(raw_far, base).reshape(STEP, HALO, K)
        mid = mid_in[rows].astype(jnp.float32)
        feat[:, 0:16] = jnp.where(odd == 0, edge, mid)

        @pl.when(odd == 0)
        def _():
            feat[:, 16:32] = mid

        @pl.when(odd == 1)
        def _():
            feat[:, 13:29] = edge

        result = compute(base, WIDE, HALO * odd, feat[...].reshape(STEP * WIDE, K), wet_far)

        @pl.when(odd == 0)
        def _():
            out_ref[rows, 0 : COLS - HALO] = result[:, : COLS - HALO]

        @pl.when(odd == 1)
        def _():
            out_ref[rows, HALO:COLS] = result[:, : COLS - HALO]

    def compute_near(c):
        base = c * STEP
        rows = pl.ds(base, STEP)
        result = compute(base, HALO, near_col, edge_features(raw_near, base), wet_near)

        @pl.when(odd == 0)
        def _():
            out_ref[rows, COLS - HALO : COLS] = result

        @pl.when(odd == 1)
        def _():
            out_ref[rows, 0:HALO] = result

    loads[0].wait()
    last = STEPS - 1
    to_rows(0)
    to_rows(last)

    @pl.when(sec == 0)
    def _():
        pl.semaphore_wait(barrier, 4)
        greet(0, partner)
        greet(1, to_near)

    @pl.when(sec == 1)
    def _():
        pl.semaphore_wait(hello.at[0], 1)

    for c in range(2):
        far_first(c).start()
        near_first(c).start()
    to_rows(1)
    far_first(2).start()

    @pl.when((sec == 1) & (lo >= EARLY))
    def _():
        meet_far()

    @pl.loop(2, last)
    def _(g):
        to_rows(g)

    far_first(3).start()
    loads[1].wait()

    @pl.loop(0, ROWS // STEP)
    def _(g):
        own = own_mid[pl.ds(g * STEP + 1, STEP)].reshape(STEP * HALO, C)
        own = silu(jnp.dot(own, cp_ref[sec], preferred_element_type=jnp.float32))
        mid_out[pl.ds(g * STEP, STEP)] = own.astype(jnp.bfloat16).reshape(STEP, HALO, K)

    loads[2].wait()
    wet = wet_ref[...].astype(jnp.float32).astype(jnp.bfloat16)
    for dst, cols, first_col in ((wet_far, WIDE, HALO * odd), (wet_near, HALO, near_col)):
        slot = first_col + lax.broadcasted_iota(jnp.int32, (cols, COLS), 0)
        slot = (slot == lax.broadcasted_iota(jnp.int32, (cols, COLS), 1)).astype(jnp.bfloat16)
        dst[...] = jnp.dot(slot, wet, preferred_element_type=jnp.float32).astype(jnp.bfloat16)
    feat[...] = jnp.zeros_like(feat)

    @pl.loop(0, (ROWS + 2) * 2)
    def _(i):
        wide[pl.ds(i * EXT + 77, 5), :] = jnp.zeros((5, 128), jnp.float32)

    for copy in loads[3:]:
        copy.wait()

    def far_ready():
        @pl.when(sec == 0)
        def _():
            pl.semaphore_wait(hello.at[2], 1)

    def far_on(c):
        relay(far_first(c), far_second(c))

    def near_on(c):
        relay(near_first(c), near_second(c))

    @pl.when(sec == 1)
    def _():
        pl.semaphore_wait(hello.at[1], 1)

    near_on(0)
    near_on(1)

    @pl.when(lo >= EARLY)
    def _():
        far_ready()
        for c in range(3):
            far_on(c)

    features_hop(0).start()
    far_first(2).wait_send()
    far_first(4).start()

    @pl.when(lo >= EARLY)
    def _():
        far_on(3)

    features_hop(1).start()
    far_first(3).wait_send()
    far_first(5).start()

    @pl.when((sec == 1) & (lo < EARLY))
    def _():
        meet_far()

    @pl.when(lo < EARLY)
    def _():
        far_ready()
        for c in range(4):
            far_on(c)

    for side, row in enumerate((1, ROWS)):
        near_second(side).wait_recv()
        widen(halo_near, near_at, row, 1)
        far_second(side).wait_recv()
        widen(halo_far, far_at, row, 1)
        for half in range(2):
            lat_out[side, 0:EXT, halves[half]] = wide[pl.ds(at(row, half, 0), EXT), :].astype(jnp.bfloat16)
        lat_hop(side).start()

    @pl.loop(0, STEPS)
    def _(c):
        @pl.when(c == 0)
        def _():
            far_on(4)
            features_hop(2).start()
            far_first(4).wait_send()
            near_first(2).start()
            lat_hop(1).wait_recv()
            lat_row(1, la > 0)

        @pl.when(c == 1)
        def _():
            far_on(5)
            features_hop(3).start()
            far_first(5).wait_send()
            near_first(3).start()

        @pl.when(c == 2)
        def _():
            near_on(2)
            near_first(2).wait_send()
            near_first(4).start()

        @pl.when(c < STEPS - 1)
        def _():
            far_second(c + 2).wait_recv()
            widen(halo_far, far_at, STEP * c + 2, STEP)

        @pl.when(c == STEPS - 1)
        def _():
            near_on(3)
            near_first(3).wait_send()
            near_first(5).start()
            far_second(CHUNKS - 1).wait_recv()
            widen(halo_far, far_at, STEP * (STEPS - 1) + 2, STEP - 2)
            lat_hop(0).wait_recv()
            lat_row(0, la < n_lat - 1)

        features_hop(c).wait_recv()
        compute_far(c)

    @pl.loop(0, STEPS)
    def _(c):
        @pl.when(c == 0)
        def _():
            near_on(4)

        @pl.when(c == 1)
        def _():
            near_on(5)

        @pl.when(c < STEPS - 1)
        def _():
            near_second(c + 2).wait_recv()
            widen(halo_near, near_at, STEP * c + 2, STEP)

        @pl.when(c == STEPS - 1)
        def _():
            near_second(CHUNKS - 1).wait_recv()
            widen(halo_near, near_at, STEP * (STEPS - 1) + 2, STEP - 2)

        compute_near(c)

    for c in range(2):
        far_first(c).wait_send()
        near_first(c).wait_send()
    near_first(4).wait_send()
    near_first(5).wait_send()
    for c in range(CHUNKS):
        far_second(c).wait_send()
        near_second(c).wait_send()
    for c in range(STEPS):
        features_hop(c).wait_send()
    lat_hop(0).wait_send()
    lat_hop(1).wait_send()


def local(state, wet_mask, tap_offsets, conv_weight, couple_proj, couple_in, norm_gain, up_weight, down_weight):
    args = (
        state[0].transpose(1, 0, 2),
        wet_mask.T,
        tap_offsets.transpose(1, 2, 0),
        conv_weight[0].reshape(TAPS * C, C),
        couple_proj,
        couple_in[0],
        norm_gain,
        up_weight[0],
        down_weight[0],
    )
    dma = pltpu.SemaphoreType.DMA
    edge = pltpu.VMEM((ROWS + 2, HALO, C), jnp.bfloat16)
    out = pl.pallas_call(
        kernel,
        out_shape=jax.ShapeDtypeStruct((ROWS, COLS, C), jnp.bfloat16),
        in_specs=[pl.BlockSpec(memory_space=pltpu.HBM)] * len(args),
        out_specs=pl.BlockSpec(memory_space=pltpu.VMEM),
        scratch_shapes=[(pltpu.SMEM if i == 2 else pltpu.VMEM)(a.shape, a.dtype) for i, a in enumerate(args)]
        + [
            pltpu.VMEM(((ROWS + 2) * 2 * EXT, 128), jnp.float32),
        ]
        + [edge] * 7
        + [
            pltpu.VMEM((2, 96, C), jnp.bfloat16),
            pltpu.VMEM((2, 96, C), jnp.bfloat16),
            pltpu.VMEM((ROWS, HALO, K), jnp.bfloat16),
            pltpu.VMEM((ROWS, HALO, K), jnp.bfloat16),
            pltpu.VMEM((STEP, WIDE, K), jnp.float32),
            pltpu.VMEM((WIDE, ROWS), jnp.bfloat16),
            pltpu.VMEM((HALO, ROWS), jnp.bfloat16),
            pltpu.VMEM((STEP * WIDE, TAPS * C), jnp.bfloat16),
            dma((len(args),)),
            dma((4, CHUNKS)),
            dma((4, CHUNKS)),
            pltpu.SemaphoreType.REGULAR((3,)),
            dma((STEPS,)),
            dma((STEPS,)),
            dma((2,)),
            dma((2,)),
        ],
        compiler_params=pltpu.CompilerParams(
            collective_id=0, has_side_effects=True, vmem_limit_bytes=62 * 1024 * 1024
        ),
        cost_estimate=pl.CostEstimate(flops=6_000_000_000, bytes_accessed=5_000_000, transcendentals=2_000_000),
    )(*args)
    return out[None]


def solution(mesh):
    in_specs = (
        P("sec", "lat", "lon", None),
        P("lat", "lon"),
        P("lat", None, None),
        P("sec", None, None, None),
        P(),
        P("sec", None, None),
        P("sec", None),
        P("sec", None, None),
        P("sec", None, None),
    )
    out_specs = P("sec", "lat", "lon", None)
    return jax.shard_map(local, mesh=mesh, in_specs=in_specs, out_specs=out_specs, check_vma=False)
```

```python
import math

import jax
import jax.numpy as jnp
from jax import lax
from jax.experimental import pallas as pl
from jax.experimental.pallas import tpu as pltpu
from jax.sharding import PartitionSpec as P

HALO = 16
ROWS = 64
COLS = 45
EXT = 82
C = 256
K = 128
HID = 512
STEP = 16
STEPS = ROWS // STEP
CHUNKS = STEPS + 2
MID = COLS - 2 * HALO
WIDE = 32
EARLY = 4
LEAD = 4
COL_UNROLL = 5
TAPS = 9
MESH = pl.DeviceIdType.MESH


def kernel(
    x_hbm,
    wet_hbm,
    off_hbm,
    cw_hbm,
    cp_hbm,
    ci_hbm,
    gain_hbm,
    up_hbm,
    down_hbm,
    out_hbm,
    x_ref,
    wet_ref,
    off_ref,
    cw_ref,
    cp_ref,
    ci_ref,
    gain_ref,
    up_ref,
    down_ref,
    wide,
    own_far,
    own_near,
    raw_far,
    raw_near,
    halo_far,
    halo_near,
    lat_out,
    lat_in,
    mid_out,
    mid_in,
    feat,
    wet_far,
    wet_near,
    picks,
    out_ref,
    load_sem,
    store_sem,
    far_sem,
    near_sem,
    hello,
    f_send,
    f_recv,
    lat_send,
    lat_recv,
):
    sec = lax.axis_index("sec")
    la = lax.axis_index("lat")
    lo = lax.axis_index("lon")
    n_lat = lax.axis_size("lat")
    n_lon = lax.axis_size("lon")
    other = 1 - sec
    odd = lax.rem(lo, 2)
    near = lo + 1 - 2 * odd
    far = lax.rem(lo + n_lon - 1 + 2 * odd, n_lon)
    north, south = lax.rem(la + n_lat - 1, n_lat), lax.rem(la + 1, n_lat)
    partner = (other, la, lo)
    to_near = (other, la, near)
    to_far = (other, la, far)
    to_north = (sec, north, lo)
    to_south = (sec, south, lo)

    barrier = pltpu.get_barrier_semaphore()

    def tell(*peers):
        for peer in peers:
            pl.semaphore_signal(barrier, inc=1, device_id=peer, device_id_type=MESH)

    def greet(i, peer):
        pl.semaphore_signal(hello.at[i], inc=1, device_id=peer, device_id_type=MESH)

    @pl.when(sec == 0)
    def _():
        tell(to_north, to_south, to_far)

    @pl.when(sec == 1)
    def _():
        tell(partner, to_near, to_north, to_south)

    def meet_far():
        pl.semaphore_wait(barrier, 3)
        greet(2, to_far)

    loads = [
        pltpu.make_async_copy(src, dst, load_sem.at[i])
        for i, (src, dst) in enumerate(
            (
                (x_hbm, x_ref),
                (cp_hbm, cp_ref),
                (wet_hbm, wet_ref),
                (off_hbm, off_ref),
                (ci_hbm, ci_ref),
                (gain_hbm, gain_ref),
                (cw_hbm, cw_ref),
                (up_hbm, up_ref),
                (down_hbm, down_ref),
            )
        )
    ]
    for copy in loads:
        copy.start()

    def rows_of(c):
        if isinstance(c, int) and c < 2:
            return pl.ds(1 if c == 0 else ROWS, 1)
        if isinstance(c, int) and c == CHUNKS - 1:
            return pl.ds(2 + STEP * (c - 2), STEP - 2)
        return pl.ds(2 + STEP * (c - 2), STEP)

    def hop(rows, src, dst, sems, first, c, target):
        return pltpu.make_async_remote_copy(
            src_ref=src.at[rows],
            dst_ref=dst.at[rows],
            send_sem=sems.at[first, c],
            recv_sem=sems.at[first + 1, c],
            device_id=target,
            device_id_type=MESH,
        )

    def far_first(c):
        return hop(rows_of(c), own_far, raw_far, far_sem, 0, c, partner)

    def far_second(c):
        return hop(rows_of(c), raw_far, halo_far, far_sem, 2, c, to_far)

    def near_first(c):
        return hop(rows_of(c), own_near, raw_near, near_sem, 0, c, partner)

    def near_second(c):
        return hop(rows_of(c), raw_near, halo_near, near_sem, 2, c, to_near)

    def features_hop(c):
        rows = pl.ds(STEP * c, STEP)
        return pltpu.make_async_remote_copy(
            src_ref=mid_out.at[:, rows],
            dst_ref=mid_in.at[:, rows],
            send_sem=f_send.at[c],
            recv_sem=f_recv.at[c],
            device_id=partner,
            device_id_type=MESH,
        )

    def lat_hop(side):
        return pltpu.make_async_remote_copy(
            src_ref=lat_out.at[side],
            dst_ref=lat_in.at[side],
            send_sem=lat_send.at[side],
            recv_sem=lat_recv.at[side],
            device_id=(to_north, to_south)[side],
            device_id_type=MESH,
        )

    def store(c):
        rows = pl.ds(STEP * c, STEP)
        return pltpu.make_async_copy(out_ref.at[rows], out_hbm.at[rows], store_sem.at[c])

    def silu(v):
        return v * (0.5 + 0.5 * jnp.tanh(0.5 * v))

    def at(row, half, col):
        return (row * 2 + half) * EXT + col

    far_col, near_col = (COLS - HALO) * odd, (COLS - HALO) * (1 - odd)
    far_at, near_at = (HALO + COLS) * odd, (HALO + COLS) * (1 - odd)
    halves = [slice(half * 128, half * 128 + 128) for half in range(2)]

    def to_rows(g):
        base = g * STEP

        @pl.loop(0, COLS, unroll=COL_UNROLL)
        def _(col):
            x = x_ref[col, pl.ds(pl.multiple_of(base, STEP), STEP)].astype(jnp.float32)
            for half in range(2):
                wide[pl.ds(at(base + 1, half, HALO + col), STEP, 2 * EXT), :] = x[:, halves[half]]

        @pl.loop(0, STEP, unroll=2)
        def _(i):
            row = base + 1 + i
            for half in range(2):
                for dst, col in ((own_far, far_col), (own_near, near_col)):
                    dst[row, :, halves[half]] = wide[pl.ds(at(row, half, HALO + col), HALO), :].astype(jnp.bfloat16)

    def widen(halo, where, start, rows):
        for row in range(rows):
            for half in range(2):
                x = halo[start + row, :, halves[half]]
                wide[pl.ds(at(start + row, half, where), HALO), :] = x.astype(jnp.float32)

    def relay(arrived, onward):
        arrived.wait_recv()
        onward.start()

    def lat_row(side, real):
        row = (ROWS + 1, 0)[side]
        for half in range(2):
            x = lat_in[side, 0:EXT, halves[half]].astype(jnp.float32)
            wide[pl.ds(at(row, half, 0), EXT), :] = jnp.where(real, x, 0.0)

    def edge_features(raw, base):
        x = raw[pl.ds(base + 1, STEP)].reshape(STEP * HALO, C)
        return silu(jnp.dot(x, cp_ref[other], preferred_element_type=jnp.float32))

    def compute(base, cols, first_col, features, wet_of):
        cells = STEP * cols

        @pl.loop(0, STEP)
        def _(i):
            start = pl.multiple_of(i * cols, 16)
            for t in range(TAPS):
                first = off_ref[t // 3, t % 3, base + i] + HALO + first_col
                for half in range(2):
                    picked = wide[pl.ds(at(base + i + t // 3, half, first), cols), :]
                    lanes = slice(t * C + half * 128, t * C + half * 128 + 128)
                    picks[pl.ds(start, cols), lanes] = picked.astype(jnp.bfloat16)

        acc = jnp.dot(picks[0:cells], cw_ref[...], preferred_element_type=jnp.float32)

        rows = lax.broadcasted_iota(jnp.int32, (ROWS, STEP * K), 0)
        lanes = lax.broadcasted_iota(jnp.int32, (ROWS, STEP * K), 1)
        spread = (rows == base + lanes // K).astype(jnp.bfloat16)
        wet = jnp.dot(wet_of[...], spread, preferred_element_type=jnp.float32)
        wet = jnp.concatenate([wet[:, i * K : (i + 1) * K] for i in range(STEP)], axis=0)
        keep_own = jnp.where(sec == 0, 0.5, 0.5 * wet)
        keep_other = jnp.where(sec == 0, wet, 1.0)

        coupled = (features * keep_other).astype(jnp.bfloat16)
        pre = acc + jnp.dot(coupled, ci_ref[...], preferred_element_type=jnp.float32)
        meansq = jnp.mean(pre * pre, axis=-1, keepdims=True)
        normed = (pre * lax.rsqrt(meansq + 1e-05) * gain_ref[...]).astype(jnp.bfloat16)
        h = jnp.dot(normed, up_ref[...], preferred_element_type=jnp.float32)
        s2p = math.sqrt(2.0 / math.pi)
        h = h + h * jnp.tanh(h * (s2p + (s2p * 0.044715) * (h * h)))
        update = jnp.dot(h.astype(jnp.bfloat16), down_ref[...], preferred_element_type=jnp.float32)
        update = update * jnp.concatenate([keep_own, keep_own], axis=1)
        field = [
            jnp.concatenate(
                [wide[pl.ds(at(base + 1 + i, half, HALO + first_col), cols), :] for i in range(STEP)], axis=0
            )
            for half in range(2)
        ]
        return (jnp.concatenate(field, axis=1) + update).astype(jnp.bfloat16).reshape(STEP, cols, C)

    def compute_far(c):
        base = c * STEP
        rows = pl.ds(base, STEP)
        edge = edge_features(raw_far, base)
        for i in range(STEP):
            feat[pl.ds(i * WIDE + MID * odd, HALO), :] = edge[i * HALO : (i + 1) * HALO]
        for col in range(MID):
            feat[pl.ds(HALO * (1 - odd) + col, STEP, WIDE), :] = mid_in[col, rows].astype(jnp.float32)
        result = compute(base, WIDE, HALO * odd, feat[...], wet_far)

        @pl.when(odd == 0)
        def _():
            out_ref[rows, 0 : COLS - HALO] = result[:, : COLS - HALO]

        @pl.when(odd == 1)
        def _():
            out_ref[rows, HALO:COLS] = result[:, : COLS - HALO]

    def compute_near(c):
        base = c * STEP
        rows = pl.ds(base, STEP)
        result = compute(base, HALO, near_col, edge_features(raw_near, base), wet_near)

        @pl.when(odd == 0)
        def _():
            out_ref[rows, COLS - HALO : COLS] = result

        @pl.when(odd == 1)
        def _():
            out_ref[rows, 0:HALO] = result

    loads[0].wait()
    last = STEPS - 1
    to_rows(0)
    to_rows(last)

    @pl.when(sec == 0)
    def _():
        pl.semaphore_wait(barrier, 4)
        greet(0, partner)
        greet(1, to_near)

    @pl.when(sec == 1)
    def _():
        pl.semaphore_wait(hello.at[0], 1)

    for c in range(2):
        far_first(c).start()
        near_first(c).start()
    to_rows(1)
    far_first(2).start()

    @pl.when((sec == 1) & (lo >= EARLY))
    def _():
        meet_far()

    @pl.loop(2, last)
    def _(g):
        to_rows(g)

    far_first(3).start()
    loads[1].wait()

    @pl.loop(0, MID)
    def _(col):
        own = jnp.dot(x_ref[HALO + col], cp_ref[sec], preferred_element_type=jnp.float32)
        mid_out[col] = silu(own).astype(jnp.bfloat16)

    loads[2].wait()
    wet = wet_ref[...].astype(jnp.float32).astype(jnp.bfloat16)
    for dst, cols, first_col in ((wet_far, WIDE, HALO * odd), (wet_near, HALO, near_col)):
        slot = first_col + lax.broadcasted_iota(jnp.int32, (cols, COLS), 0)
        slot = (slot == lax.broadcasted_iota(jnp.int32, (cols, COLS), 1)).astype(jnp.bfloat16)
        dst[...] = jnp.dot(slot, wet, preferred_element_type=jnp.float32).astype(jnp.bfloat16)
    feat[...] = jnp.zeros_like(feat)

    @pl.loop(0, (ROWS + 2) * 2)
    def _(i):
        wide[pl.ds(i * EXT + 77, 5), :] = jnp.zeros((5, 128), jnp.float32)

    for copy in loads[3:]:
        copy.wait()

    def far_ready():
        @pl.when(sec == 0)
        def _():
            pl.semaphore_wait(hello.at[2], 1)

    def far_on(c):
        relay(far_first(c), far_second(c))

    def near_on(c):
        relay(near_first(c), near_second(c))

    @pl.when(sec == 1)
    def _():
        pl.semaphore_wait(hello.at[1], 1)

    near_on(0)
    near_on(1)

    @pl.when(lo >= EARLY)
    def _():
        far_ready()
        for c in range(3):
            far_on(c)

    far_first(2).wait_send()
    far_first(4).start()

    @pl.when(lo >= EARLY)
    def _():
        far_on(3)

    far_first(3).wait_send()
    far_first(5).start()

    @pl.when((sec == 1) & (lo < EARLY))
    def _():
        meet_far()

    @pl.when(lo < EARLY)
    def _():
        far_ready()
        for c in range(4):
            far_on(c)

    far_on(4)
    far_first(4).wait_send()
    features_hop(0).start()
    features_hop(1).start()

    far_on(5)
    far_first(5).wait_send()
    features_hop(2).start()
    features_hop(3).start()

    for side, row in enumerate((1, ROWS)):
        near_second(side).wait_recv()
        widen(halo_near, near_at, row, 1)
        far_second(side).wait_recv()
        widen(halo_far, far_at, row, 1)
        for half in range(2):
            lat_out[side, 0:EXT, halves[half]] = wide[pl.ds(at(row, half, 0), EXT), :].astype(jnp.bfloat16)
        lat_hop(side).start()

    @pl.loop(0, STEPS)
    def _(c):
        @pl.when(c == 0)
        def _():
            near_first(2).start()
            lat_hop(1).wait_recv()
            lat_row(1, la > 0)

        @pl.when(c == 1)
        def _():
            near_first(3).start()

        @pl.when(c == 2)
        def _():
            near_on(2)
            near_first(2).wait_send()
            near_first(4).start()

        @pl.when(c < STEPS - 1)
        def _():
            far_second(c + 2).wait_recv()
            widen(halo_far, far_at, STEP * c + 2, STEP)

        @pl.when(c == STEPS - 1)
        def _():
            near_on(3)
            near_first(3).wait_send()
            near_first(5).start()
            far_second(CHUNKS - 1).wait_recv()
            widen(halo_far, far_at, STEP * (STEPS - 1) + 2, STEP - 2)
            lat_hop(0).wait_recv()
            lat_row(0, la < n_lat - 1)

        features_hop(c).wait_recv()
        compute_far(c)

    @pl.loop(0, STEPS)
    def _(c):
        @pl.when(c == 0)
        def _():
            near_on(4)

        @pl.when(c == 1)
        def _():
            near_on(5)

        @pl.when(c < STEPS - 1)
        def _():
            near_second(c + 2).wait_recv()
            widen(halo_near, near_at, STEP * c + 2, STEP)

        @pl.when(c == STEPS - 1)
        def _():
            near_second(CHUNKS - 1).wait_recv()
            widen(halo_near, near_at, STEP * (STEPS - 1) + 2, STEP - 2)

        compute_near(c)
        store(c).start()

    for c in range(2):
        far_first(c).wait_send()
        near_first(c).wait_send()
    near_first(4).wait_send()
    near_first(5).wait_send()
    for c in range(CHUNKS):
        far_second(c).wait_send()
        near_second(c).wait_send()
    for c in range(STEPS):
        features_hop(c).wait_send()
    lat_hop(0).wait_send()
    lat_hop(1).wait_send()
    for c in range(STEPS):
        store(c).wait()


def local(state, wet_mask, tap_offsets, conv_weight, couple_proj, couple_in, norm_gain, up_weight, down_weight):
    args = (
        state[0].transpose(1, 0, 2),
        wet_mask.T,
        tap_offsets.transpose(1, 2, 0),
        conv_weight[0].reshape(TAPS * C, C),
        couple_proj,
        couple_in[0],
        norm_gain,
        up_weight[0],
        down_weight[0],
    )
    dma = pltpu.SemaphoreType.DMA
    edge = pltpu.VMEM((ROWS + 2, HALO, C), jnp.bfloat16)
    out = pl.pallas_call(
        kernel,
        out_shape=jax.ShapeDtypeStruct((ROWS, COLS, C), jnp.bfloat16),
        in_specs=[pl.BlockSpec(memory_space=pltpu.HBM)] * len(args),
        out_specs=pl.BlockSpec(memory_space=pl.ANY),
        scratch_shapes=[(pltpu.SMEM if i == 2 else pltpu.VMEM)(a.shape, a.dtype) for i, a in enumerate(args)]
        + [
            pltpu.VMEM(((ROWS + 2) * 2 * EXT, 128), jnp.float32),
        ]
        + [edge] * 6
        + [
            pltpu.VMEM((2, 96, C), jnp.bfloat16),
            pltpu.VMEM((2, 96, C), jnp.bfloat16),
            pltpu.VMEM((MID, ROWS, K), jnp.bfloat16),
            pltpu.VMEM((MID, ROWS, K), jnp.bfloat16),
            pltpu.VMEM((STEP * WIDE, K), jnp.float32),
            pltpu.VMEM((WIDE, ROWS), jnp.bfloat16),
            pltpu.VMEM((HALO, ROWS), jnp.bfloat16),
            pltpu.VMEM((STEP * WIDE, TAPS * C), jnp.bfloat16),
            pltpu.VMEM((ROWS, COLS, C), jnp.bfloat16),
            dma((len(args),)),
            dma((STEPS,)),
            dma((4, CHUNKS)),
            dma((4, CHUNKS)),
            pltpu.SemaphoreType.REGULAR((3,)),
            dma((STEPS,)),
            dma((STEPS,)),
            dma((2,)),
            dma((2,)),
        ],
        compiler_params=pltpu.CompilerParams(
            collective_id=0, has_side_effects=True, vmem_limit_bytes=62 * 1024 * 1024
        ),
        cost_estimate=pl.CostEstimate(flops=6_000_000_000, bytes_accessed=5_000_000, transcendentals=2_000_000),
    )(*args)
    return out[None]


def solution(mesh):
    in_specs = (
        P("sec", "lat", "lon", None),
        P("lat", "lon"),
        P("lat", None, None),
        P("sec", None, None, None),
        P(),
        P("sec", None, None),
        P("sec", None),
        P("sec", None, None),
        P("sec", None, None),
    )
    out_specs = P("sec", "lat", "lon", None)
    return jax.shard_map(local, mesh=mesh, in_specs=in_specs, out_specs=out_specs, check_vma=False)
```

```python
import math

import jax
import jax.numpy as jnp
from jax import lax
from jax.experimental import pallas as pl
from jax.experimental.pallas import tpu as pltpu
from jax.sharding import PartitionSpec as P

HALO = 16
ROWS = 64
COLS = 45
EXT = 82
C = 256
K = 128
HID = 512
STEP = 16
STEPS = ROWS // STEP
CHUNKS = STEPS + 2
MID = COLS - 2 * HALO
WIDE = 32
EARLY = 4
LEAD = 4
COL_UNROLL = 5
TAPS = 9
MESH = pl.DeviceIdType.MESH


def kernel(
    x_hbm,
    wet_hbm,
    off_hbm,
    cw_hbm,
    cp_hbm,
    ci_hbm,
    gain_hbm,
    up_hbm,
    down_hbm,
    out_hbm,
    x_ref,
    wet_ref,
    off_ref,
    cw_ref,
    cp_ref,
    ci_ref,
    gain_ref,
    up_ref,
    down_ref,
    wide,
    own_far,
    own_near,
    raw_far,
    raw_near,
    halo_far,
    halo_near,
    lat_out,
    lat_in,
    mid_out,
    mid_in,
    feat,
    wet_far,
    wet_near,
    picks,
    out_ref,
    load_sem,
    store_sem,
    far_sem,
    near_sem,
    hello,
    f_send,
    f_recv,
    lat_send,
    lat_recv,
):
    sec = lax.axis_index("sec")
    la = lax.axis_index("lat")
    lo = lax.axis_index("lon")
    n_lat = lax.axis_size("lat")
    n_lon = lax.axis_size("lon")
    other = 1 - sec
    odd = lax.rem(lo, 2)
    near = lo + 1 - 2 * odd
    far = lax.rem(lo + n_lon - 1 + 2 * odd, n_lon)
    north, south = lax.rem(la + n_lat - 1, n_lat), lax.rem(la + 1, n_lat)
    partner = (other, la, lo)
    to_near = (other, la, near)
    to_far = (other, la, far)
    to_north = (sec, north, lo)
    to_south = (sec, south, lo)

    barrier = pltpu.get_barrier_semaphore()

    def tell(*peers):
        for peer in peers:
            pl.semaphore_signal(barrier, inc=1, device_id=peer, device_id_type=MESH)

    def greet(i, peer):
        pl.semaphore_signal(hello.at[i], inc=1, device_id=peer, device_id_type=MESH)

    @pl.when(sec == 0)
    def _():
        tell(to_north, to_south, to_far)

    @pl.when(sec == 1)
    def _():
        tell(partner, to_near, to_north, to_south)

    def meet_far():
        pl.semaphore_wait(barrier, 3)
        greet(2, to_far)

    loads = [
        pltpu.make_async_copy(src, dst, load_sem.at[i])
        for i, (src, dst) in enumerate(
            (
                (x_hbm, x_ref),
                (cp_hbm, cp_ref),
                (wet_hbm, wet_ref),
                (off_hbm, off_ref),
                (ci_hbm, ci_ref),
                (gain_hbm, gain_ref),
                (cw_hbm, cw_ref),
                (up_hbm, up_ref),
                (down_hbm, down_ref),
            )
        )
    ]
    for copy in loads:
        copy.start()

    def rows_of(c):
        if isinstance(c, int) and c < 2:
            return pl.ds(1 if c == 0 else ROWS, 1)
        if isinstance(c, int) and c == CHUNKS - 1:
            return pl.ds(2 + STEP * (c - 2), STEP - 2)
        return pl.ds(2 + STEP * (c - 2), STEP)

    def hop(rows, src, dst, sems, first, c, target):
        return pltpu.make_async_remote_copy(
            src_ref=src.at[rows],
            dst_ref=dst.at[rows],
            send_sem=sems.at[first, c],
            recv_sem=sems.at[first + 1, c],
            device_id=target,
            device_id_type=MESH,
        )

    def far_first(c):
        return hop(rows_of(c), own_far, raw_far, far_sem, 0, c, partner)

    def far_second(c):
        return hop(rows_of(c), raw_far, halo_far, far_sem, 2, c, to_far)

    def near_first(c):
        return hop(rows_of(c), own_near, raw_near, near_sem, 0, c, partner)

    def near_second(c):
        return hop(rows_of(c), raw_near, halo_near, near_sem, 2, c, to_near)

    def features_hop(c):
        rows = pl.ds(STEP * c, STEP)
        return pltpu.make_async_remote_copy(
            src_ref=mid_out.at[:, rows],
            dst_ref=mid_in.at[:, rows],
            send_sem=f_send.at[c],
            recv_sem=f_recv.at[c],
            device_id=partner,
            device_id_type=MESH,
        )

    def lat_hop(side):
        return pltpu.make_async_remote_copy(
            src_ref=lat_out.at[side],
            dst_ref=lat_in.at[side],
            send_sem=lat_send.at[side],
            recv_sem=lat_recv.at[side],
            device_id=(to_north, to_south)[side],
            device_id_type=MESH,
        )

    def store(c):
        rows = pl.ds(STEP * c, STEP)
        return pltpu.make_async_copy(out_ref.at[rows], out_hbm.at[rows], store_sem.at[c])

    def silu(v):
        return v * (0.5 + 0.5 * jnp.tanh(0.5 * v))

    def at(row, half, col):
        return (row * 2 + half) * EXT + col

    far_col, near_col = (COLS - HALO) * odd, (COLS - HALO) * (1 - odd)
    far_at, near_at = (HALO + COLS) * odd, (HALO + COLS) * (1 - odd)
    halves = [slice(half * 128, half * 128 + 128) for half in range(2)]

    def to_rows(g):
        base = g * STEP

        @pl.loop(0, COLS, unroll=COL_UNROLL)
        def _(col):
            x = x_ref[col, pl.ds(pl.multiple_of(base, STEP), STEP)].astype(jnp.float32)
            for half in range(2):
                wide[pl.ds(at(base + 1, half, HALO + col), STEP, 2 * EXT), :] = x[:, halves[half]]

        @pl.loop(0, STEP, unroll=2)
        def _(i):
            row = base + 1 + i
            for half in range(2):
                for dst, col in ((own_far, far_col), (own_near, near_col)):
                    dst[row, :, halves[half]] = wide[pl.ds(at(row, half, HALO + col), HALO), :].astype(jnp.bfloat16)

    def widen(halo, where, start, rows):
        for row in range(rows):
            for half in range(2):
                x = halo[start + row, :, halves[half]]
                wide[pl.ds(at(start + row, half, where), HALO), :] = x.astype(jnp.float32)

    def relay(arrived, onward):
        arrived.wait_recv()
        onward.start()

    def lat_row(side, real):
        row = (ROWS + 1, 0)[side]
        for half in range(2):
            x = lat_in[side, 0:EXT, halves[half]].astype(jnp.float32)
            wide[pl.ds(at(row, half, 0), EXT), :] = jnp.where(real, x, 0.0)

    def edge_features(raw, base):
        x = raw[pl.ds(base + 1, STEP)].reshape(STEP * HALO, C)
        return silu(jnp.dot(x, cp_ref[other], preferred_element_type=jnp.float32))

    def compute(base, cols, first_col, features, wet_of):
        cells = STEP * cols

        @pl.loop(0, STEP)
        def _(i):
            start = pl.multiple_of(i * cols, 16)
            for t in range(TAPS):
                first = off_ref[t // 3, t % 3, base + i] + HALO + first_col
                for half in range(2):
                    picked = wide[pl.ds(at(base + i + t // 3, half, first), cols), :]
                    lanes = slice(t * C + half * 128, t * C + half * 128 + 128)
                    picks[pl.ds(start, cols), lanes] = picked.astype(jnp.bfloat16)

        acc = jnp.dot(picks[0:cells], cw_ref[...], preferred_element_type=jnp.float32)

        rows = lax.broadcasted_iota(jnp.int32, (ROWS, STEP * K), 0)
        lanes = lax.broadcasted_iota(jnp.int32, (ROWS, STEP * K), 1)
        spread = (rows == base + lanes // K).astype(jnp.bfloat16)
        wet = jnp.dot(wet_of[...], spread, preferred_element_type=jnp.float32)
        wet = jnp.concatenate([wet[:, i * K : (i + 1) * K] for i in range(STEP)], axis=0)
        keep_own = jnp.where(sec == 0, 0.5, 0.5 * wet)
        keep_other = jnp.where(sec == 0, wet, 1.0)

        coupled = (features * keep_other).astype(jnp.bfloat16)
        pre = acc + jnp.dot(coupled, ci_ref[...], preferred_element_type=jnp.float32)
        meansq = jnp.mean(pre * pre, axis=-1, keepdims=True)
        normed = (pre * lax.rsqrt(meansq + 1e-05) * gain_ref[...]).astype(jnp.bfloat16)
        h = jnp.dot(normed, up_ref[...], preferred_element_type=jnp.float32)
        s2p = math.sqrt(2.0 / math.pi)
        h = h + h * jnp.tanh(h * (s2p + (s2p * 0.044715) * (h * h)))
        update = jnp.dot(h.astype(jnp.bfloat16), down_ref[...], preferred_element_type=jnp.float32)
        update = update * jnp.concatenate([keep_own, keep_own], axis=1)
        field = [
            jnp.concatenate(
                [wide[pl.ds(at(base + 1 + i, half, HALO + first_col), cols), :] for i in range(STEP)], axis=0
            )
            for half in range(2)
        ]
        return (jnp.concatenate(field, axis=1) + update).astype(jnp.bfloat16).reshape(STEP, cols, C)

    def compute_far(c):
        base = c * STEP
        rows = pl.ds(base, STEP)
        edge = edge_features(raw_far, base)
        for i in range(STEP):
            feat[pl.ds(i * WIDE + MID * odd, HALO), :] = edge[i * HALO : (i + 1) * HALO]
        for col in range(MID):
            feat[pl.ds(HALO * (1 - odd) + col, STEP, WIDE), :] = mid_in[col, rows].astype(jnp.float32)
        result = compute(base, WIDE, HALO * odd, feat[...], wet_far)

        @pl.when(odd == 0)
        def _():
            out_ref[rows, 0 : COLS - HALO] = result[:, : COLS - HALO]

        @pl.when(odd == 1)
        def _():
            out_ref[rows, HALO:COLS] = result[:, : COLS - HALO]

    def compute_near(c):
        base = c * STEP
        rows = pl.ds(base, STEP)
        result = compute(base, HALO, near_col, edge_features(raw_near, base), wet_near)

        @pl.when(odd == 0)
        def _():
            out_ref[rows, COLS - HALO : COLS] = result

        @pl.when(odd == 1)
        def _():
            out_ref[rows, 0:HALO] = result

    loads[0].wait()
    last = STEPS - 1
    to_rows(0)
    to_rows(last)

    @pl.when((sec == 1) & (lo >= EARLY))
    def _():
        meet_far()

    @pl.when(sec == 0)
    def _():
        pl.semaphore_wait(barrier, 4)
        greet(0, partner)
        greet(1, to_near)

    @pl.when(sec == 1)
    def _():
        pl.semaphore_wait(hello.at[0], 1)

    for c in range(2):
        far_first(c).start()
        near_first(c).start()
    to_rows(1)
    far_first(2).start()

    @pl.loop(2, last)
    def _(g):
        to_rows(g)

    far_first(3).start()
    loads[1].wait()

    @pl.loop(0, MID)
    def _(col):
        own = jnp.dot(x_ref[HALO + col], cp_ref[sec], preferred_element_type=jnp.float32)
        mid_out[col] = silu(own).astype(jnp.bfloat16)

    loads[2].wait()
    wet = wet_ref[...].astype(jnp.float32).astype(jnp.bfloat16)
    for dst, cols, first_col in ((wet_far, WIDE, HALO * odd), (wet_near, HALO, near_col)):
        slot = first_col + lax.broadcasted_iota(jnp.int32, (cols, COLS), 0)
        slot = (slot == lax.broadcasted_iota(jnp.int32, (cols, COLS), 1)).astype(jnp.bfloat16)
        dst[...] = jnp.dot(slot, wet, preferred_element_type=jnp.float32).astype(jnp.bfloat16)
    feat[...] = jnp.zeros_like(feat)

    @pl.loop(0, (ROWS + 2) * 2)
    def _(i):
        wide[pl.ds(i * EXT + 77, 5), :] = jnp.zeros((5, 128), jnp.float32)

    for copy in loads[3:]:
        copy.wait()

    def far_ready():
        @pl.when(sec == 0)
        def _():
            pl.semaphore_wait(hello.at[2], 1)

    def far_on(c):
        relay(far_first(c), far_second(c))

    def near_on(c):
        relay(near_first(c), near_second(c))

    @pl.when(sec == 1)
    def _():
        pl.semaphore_wait(hello.at[1], 1)

    near_on(0)
    near_on(1)

    @pl.when(lo >= EARLY)
    def _():
        far_ready()
        for c in range(3):
            far_on(c)

    far_first(2).wait_send()
    far_first(4).start()

    @pl.when(lo >= EARLY)
    def _():
        far_on(3)

    far_first(3).wait_send()
    far_first(5).start()

    @pl.when((sec == 1) & (lo < EARLY))
    def _():
        meet_far()

    @pl.when(lo < EARLY)
    def _():
        far_ready()
        for c in range(4):
            far_on(c)

    far_on(4)
    far_first(4).wait_send()
    features_hop(0).start()
    features_hop(1).start()

    far_on(5)
    far_first(5).wait_send()
    features_hop(2).start()
    features_hop(3).start()

    for side, row in enumerate((1, ROWS)):
        near_second(side).wait_recv()
        widen(halo_near, near_at, row, 1)
        far_second(side).wait_recv()
        widen(halo_far, far_at, row, 1)
        for half in range(2):
            lat_out[side, 0:EXT, halves[half]] = wide[pl.ds(at(row, half, 0), EXT), :].astype(jnp.bfloat16)
        lat_hop(side).start()

    @pl.loop(0, STEPS)
    def _(c):
        @pl.when(c == 0)
        def _():
            near_first(2).start()
            lat_hop(1).wait_recv()
            lat_row(1, la > 0)

        @pl.when(c == 1)
        def _():
            near_first(3).start()

        @pl.when(c == 2)
        def _():
            near_on(2)
            near_first(2).wait_send()
            near_first(4).start()

        @pl.when(c < STEPS - 1)
        def _():
            far_second(c + 2).wait_recv()
            widen(halo_far, far_at, STEP * c + 2, STEP)

        @pl.when(c == STEPS - 1)
        def _():
            near_on(3)
            near_first(3).wait_send()
            near_first(5).start()
            far_second(CHUNKS - 1).wait_recv()
            widen(halo_far, far_at, STEP * (STEPS - 1) + 2, STEP - 2)
            lat_hop(0).wait_recv()
            lat_row(0, la < n_lat - 1)

        features_hop(c).wait_recv()
        compute_far(c)

    @pl.loop(0, STEPS)
    def _(c):
        @pl.when(c == 0)
        def _():
            near_on(4)

        @pl.when(c == 1)
        def _():
            near_on(5)

        @pl.when(c < STEPS - 1)
        def _():
            near_second(c + 2).wait_recv()
            widen(halo_near, near_at, STEP * c + 2, STEP)

        @pl.when(c == STEPS - 1)
        def _():
            near_second(CHUNKS - 1).wait_recv()
            widen(halo_near, near_at, STEP * (STEPS - 1) + 2, STEP - 2)

        compute_near(c)
        store(c).start()

    for c in range(2):
        far_first(c).wait_send()
        near_first(c).wait_send()
    near_first(4).wait_send()
    near_first(5).wait_send()
    for c in range(CHUNKS):
        far_second(c).wait_send()
        near_second(c).wait_send()
    for c in range(STEPS):
        features_hop(c).wait_send()
    lat_hop(0).wait_send()
    lat_hop(1).wait_send()
    for c in range(STEPS):
        store(c).wait()


def local(state, wet_mask, tap_offsets, conv_weight, couple_proj, couple_in, norm_gain, up_weight, down_weight):
    args = (
        state[0].transpose(1, 0, 2),
        wet_mask.T,
        tap_offsets.transpose(1, 2, 0),
        conv_weight[0].reshape(TAPS * C, C),
        couple_proj,
        couple_in[0],
        norm_gain,
        up_weight[0],
        down_weight[0],
    )
    dma = pltpu.SemaphoreType.DMA
    edge = pltpu.VMEM((ROWS + 2, HALO, C), jnp.bfloat16)
    out = pl.pallas_call(
        kernel,
        out_shape=jax.ShapeDtypeStruct((ROWS, COLS, C), jnp.bfloat16),
        in_specs=[pl.BlockSpec(memory_space=pltpu.HBM)] * len(args),
        out_specs=pl.BlockSpec(memory_space=pl.ANY),
        scratch_shapes=[(pltpu.SMEM if i == 2 else pltpu.VMEM)(a.shape, a.dtype) for i, a in enumerate(args)]
        + [
            pltpu.VMEM(((ROWS + 2) * 2 * EXT, 128), jnp.float32),
        ]
        + [edge] * 6
        + [
            pltpu.VMEM((2, 96, C), jnp.bfloat16),
            pltpu.VMEM((2, 96, C), jnp.bfloat16),
            pltpu.VMEM((MID, ROWS, K), jnp.bfloat16),
            pltpu.VMEM((MID, ROWS, K), jnp.bfloat16),
            pltpu.VMEM((STEP * WIDE, K), jnp.float32),
            pltpu.VMEM((WIDE, ROWS), jnp.bfloat16),
            pltpu.VMEM((HALO, ROWS), jnp.bfloat16),
            pltpu.VMEM((STEP * WIDE, TAPS * C), jnp.bfloat16),
            pltpu.VMEM((ROWS, COLS, C), jnp.bfloat16),
            dma((len(args),)),
            dma((STEPS,)),
            dma((4, CHUNKS)),
            dma((4, CHUNKS)),
            pltpu.SemaphoreType.REGULAR((3,)),
            dma((STEPS,)),
            dma((STEPS,)),
            dma((2,)),
            dma((2,)),
        ],
        compiler_params=pltpu.CompilerParams(
            collective_id=0, has_side_effects=True, vmem_limit_bytes=62 * 1024 * 1024
        ),
        cost_estimate=pl.CostEstimate(flops=6_000_000_000, bytes_accessed=5_000_000, transcendentals=2_000_000),
    )(*args)
    return out[None]


def solution(mesh):
    in_specs = (
        P("sec", "lat", "lon", None),
        P("lat", "lon"),
        P("lat", None, None),
        P("sec", None, None, None),
        P(),
        P("sec", None, None),
        P("sec", None),
        P("sec", None, None),
        P("sec", None, None),
    )
    out_specs = P("sec", "lat", "lon", None)
    return jax.shard_map(local, mesh=mesh, in_specs=in_specs, out_specs=out_specs, check_vma=False)
```
